256 devices in a mesh: dom: 32 (over y, z_lo, x), rep: 8 (over z_hi, core).
Axes of the slice: x: 4, y: 4, z: 8 (z_hi: 4, z_lo: 2; z = z_hi * 2 + z_lo), core: 2. Of those that a mesh axis runs over, the one named last changes fastest.
Arguments:
- codes: bfloat16 [65536, 256], P('dom'), may hold values from -1.5 to 1.5
- scales: bfloat16 [65536], P('dom'), may hold values from 0.5 to 2
- accum: float32 [65536], P('dom'), may hold values from 0.01 to 1
- relations: bfloat16 [64, 256], replicated, may hold values from -5 to 5
- matching: int32 [32], P('dom'), may hold values from 0 to 31, as said below
- edges: int32 [3, 1048576], P(None, ('dom', 'rep')), may hold values from 0 to 2047, as said below
- counts: int32 [256], P(('dom', 'rep')), may hold values from 1 to 4096, 524288 in all
- negatives: int32 [2048, 1024], P(('dom', 'rep')), may hold values from 0 to 2047
Outputs:
- new_codes: bfloat16 [65536, 256], P('dom')
- new_accum: float32 [65536], P(('dom', 'rep'))
The draws below stay inside these ranges and needn't reach their ends.
Inputs may be any that keep to these rules, and one draw needn't show every extreme that they name: matching[b] = b XOR m for one m from 1 to 31 shared by all buckets, so partitions pair up. `edges`: rows 0 and 2 hold row ids below 2048, row 1 relation ids below 64.
All inputs are finite; a program needn't handle non-finite values. No bound on the sum of `counts` on one device may be relied on, other than what follows from the above.
Results may differ from the reference program's by a relative error of at most 0.0075.
Values may be sent and summed in bfloat16 or wider, within the bound.
A program may use at most 64 MiB of HBM per device.

```python
import math
import jax
import jax.numpy as jnp
import numpy as np
from jax import lax

D = 256
P_ROWS = 2048
GROUP = 512
NEG = 1024
CH_DEV = 8
REL = 64
PARTITIONS = 32
EDGE_SHARDS = 256
EDGES_DEV = 4096
EDGES = 1048576
GROUPS = 2048
ENTITIES = 65536
N_REP = 8


def draw_edges(key, part):
    key = jax.random.fold_in(key, 11)
    key_src, key_rel, key_dst = jax.random.split(key, 3)
    source = jax.random.randint(key_src, (EDGES,), 0, P_ROWS)
    relation = jax.random.randint(key_rel, (EDGES,), 0, REL)
    target = jax.random.randint(key_dst, (EDGES,), 0, P_ROWS)
    slot_pos = jnp.arange(EDGES)
    source = jnp.where(slot_pos == 0, P_ROWS - 1, source)
    target = jnp.where(slot_pos == 0, 0, target)
    return jnp.stack([source, relation, target]).astype(jnp.int32)


def draw_matching(key, part):
    key = jax.random.fold_in(key, 12)
    offset = jax.random.randint(key, (), 1, PARTITIONS)
    return jnp.bitwise_xor(jnp.arange(PARTITIONS, dtype=jnp.int32), offset.astype(jnp.int32))


def set_ends(drawn, stream_key, smallest, top_value):
    spot = [jax.random.randint(jax.random.fold_in(stream_key, axis), (), 0, length) for axis, length in enumerate(drawn.shape)]
    longest = drawn.shape.index(max(drawn.shape))
    neighbour = spot[:longest] + [(spot[longest] + 1) % drawn.shape[longest]] + spot[longest + 1:]
    return drawn.at[tuple(spot)].set(smallest).at[tuple(neighbour)].set(top_value)


def block_scale(own_key, extent, cuts, low, high):
    factor_of = 1.0
    for dim, parts in cuts:
        draws = jax.random.uniform(jax.random.fold_in(jax.random.fold_in(own_key, 6), dim), (parts,), jnp.float32, low / len(cuts), high / len(cuts))
        factor_of = factor_of * jnp.repeat(jnp.exp(draws), extent[dim] // parts).reshape((-1,) + (1,) * (len(extent) - 1 - dim))
    return factor_of


def split_up(count, total, most, skew):
    portions = [(1 << 20) // math.isqrt(grade ** skew) + 1 for grade in range(2, count + 1)]
    rest, holding = total - most - (count - 1), [1] * (count - 1)
    while rest > 0:
        free = [i for i in range(count - 1) if holding[i] < most]
        mass, budget = sum([portions[i] for i in free]), rest
        for i in free:
            more = min(most - holding[i], max(1, budget * portions[i] // mass), rest)
            holding[i] = holding[i] + more
            rest = rest - more
    return np.array([most] + holding)


def uneven(key, number_of, total, bound, slope):
    if number_of == 2:
        one = jax.random.randint(key, (), max(1, total - bound), min(bound, total - 1) + 1)
        return jnp.stack([one, total - one])
    sizes = jnp.asarray(split_up(number_of, total, bound, slope), jnp.int32)
    twos = (number_of - 1) // 2
    donor, sink = sizes[1:1 + 2 * twos:2], sizes[2:2 + 2 * twos:2]
    room = jnp.minimum(donor - 1, bound - sink)
    shifted = jax.random.randint(jax.random.fold_in(key, 1), (twos,), 0, 1 << 20) % (room + 1)
    sizes = sizes.at[1:1 + 2 * twos:2].set(donor - shifted).at[2:2 + 2 * twos:2].set(sink + shifted)
    return sizes[jax.random.permutation(jax.random.fold_in(key, 2), number_of)]


def bell_draw(rng, dims, scale, reach, pieces=(), held_as=jnp.bfloat16):
    loudness = block_scale(rng, dims, pieces, -0.22, 0.18) if pieces else 1.0
    entries = jax.random.normal(rng, dims, jnp.float32) * scale * loudness
    return jnp.minimum(jnp.maximum(entries, -reach), reach).astype(held_as)


def setup_inputs(seed: int = 0) -> dict:
    splits = jax.random.split(jax.random.key(seed), 9)
    codes = bell_draw(splits[0], (ENTITIES, D), 0.25, 1.5, ((0, 32),))
    scales = jnp.clip(jnp.exp(math.log(2.0) - 1.3862944 * jax.random.uniform(splits[1], (ENTITIES,), jnp.float32) ** block_scale(splits[1], (ENTITIES,), ((0, 32),), -0.2, 0.2)), 0.5, 2.0).astype(jnp.bfloat16)
    accum = jnp.clip(jnp.exp(math.log(1.0) - 4.6051702 * jax.random.uniform(splits[2], (ENTITIES,), jnp.float32) ** block_scale(splits[2], (ENTITIES,), ((0, 32),), -0.2, 0.2)), 0.01, 1.0)
    relations = bell_draw(splits[3], (REL, D), 1.0, 5.0)
    matching = draw_matching(jax.random.fold_in(splits[8], 71), 0)
    edges = draw_edges(jax.random.fold_in(splits[8], 71), 0)
    counts = uneven(splits[6], EDGE_SHARDS, EDGES_DEV * EDGE_SHARDS // 2, EDGES_DEV, 2).astype(jnp.int32)
    negatives = set_ends(jax.random.randint(splits[7], (GROUPS, NEG), 0, P_ROWS), jax.random.fold_in(splits[7], 1), 0, P_ROWS - 1).astype(jnp.int32)
    return {"codes": codes, "scales": scales, "accum": accum, "relations": relations, "matching": matching, "edges": edges, "counts": counts, "negatives": negatives}


LEARN_RATE = 0.1
ROOT_EPSILON = 1e-08

def group_terms(src_block, dst_block, relation_rows, src_ids, dst_ids, live_mask, negative_ids):
    source_rows = jnp.take(src_block, src_ids, axis=0).astype(jnp.float32)
    target_rows = jnp.take(dst_block, dst_ids, axis=0)
    negative_rows = jnp.take(dst_block, negative_ids, axis=0)
    relation_f = relation_rows.astype(jnp.float32)
    query = (source_rows * relation_f).astype(jnp.bfloat16)
    positive = lax.optimization_barrier(jnp.sum(query.astype(jnp.float32) * target_rows.astype(jnp.float32), axis=1))
    scores = jnp.dot(query, negative_rows.T, preferred_element_type=jnp.float32)
    weight = live_mask.astype(jnp.float32)
    pos_coef = -weight * jax.nn.sigmoid(-positive)
    neg_coef = (weight[:, None] * jax.nn.sigmoid(scores) / negative_rows.shape[0]).astype(jnp.bfloat16)
    query_grad = pos_coef[:, None] * target_rows.astype(jnp.float32) + jnp.dot(neg_coef, negative_rows, preferred_element_type=jnp.float32)
    source_grad = query_grad * relation_f
    target_grad = pos_coef[:, None] * query.astype(jnp.float32)
    negative_grad = jnp.dot(neg_coef.T, query, preferred_element_type=jnp.float32)
    return (source_grad, target_grad, negative_grad)

def reference(codes, scales, accum, relations, matching, edges, counts, negatives):
    values = codes.astype(jnp.float32) * scales.astype(jnp.float32)[:, None]
    rounded = values.astype(jnp.bfloat16).reshape(PARTITIONS, P_ROWS, D)
    per_bucket = N_REP * CH_DEV
    edge_ids = edges.reshape(3, PARTITIONS, per_bucket, GROUP)
    slot_pos = jnp.arange(EDGES_DEV, dtype=jnp.int32)
    live_all = (slot_pos[None, :] < counts[:, None]).astype(jnp.int32).reshape(PARTITIONS, per_bucket, GROUP)
    neg_all = negatives.reshape(PARTITIONS, per_bucket, NEG)

    def bucket(gradients, owner):
        partner = matching[owner]
        src_block = rounded[owner]
        dst_block = rounded[partner]

        def group_step(carry, group_at):
            src_ids = edge_ids[0, owner, group_at]
            rel_ids = edge_ids[1, owner, group_at]
            dst_ids = edge_ids[2, owner, group_at]
            live_mask = live_all[owner, group_at]
            negative_ids = neg_all[owner, group_at]

            def score_group(grads_in):
                relation_rows = jnp.take(relations, rel_ids, axis=0)
                source_grad, target_grad, negative_grad = group_terms(src_block, dst_block, relation_rows, src_ids, dst_ids, live_mask, negative_ids)
                first = grads_in[0].at[src_ids].add(source_grad)
                second = grads_in[1].at[dst_ids].add(target_grad).at[negative_ids].add(negative_grad)
                return (first, second)
            result = lax.cond(jnp.any(live_mask > 0), score_group, lambda grads_in: grads_in, carry)
            return (result, None)
        empty = jnp.zeros((P_ROWS, D), jnp.float32)
        (src_total, dst_total), _ = lax.scan(group_step, (empty, empty), jnp.arange(per_bucket, dtype=jnp.int32))
        gradients = gradients.at[owner].add(src_total).at[partner].add(dst_total)
        return (gradients, None)
    start_grads = jnp.zeros((PARTITIONS, P_ROWS, D), jnp.float32)
    grad_all, _ = lax.scan(bucket, start_grads, jnp.arange(PARTITIONS, dtype=jnp.int32))
    grad_all = grad_all.reshape(ENTITIES, D)
    new_accum = accum + lax.optimization_barrier(jnp.mean(grad_all * grad_all, axis=1))
    updated = values - LEARN_RATE * grad_all / (jnp.sqrt(new_accum)[:, None] + ROOT_EPSILON)
    new_codes = (updated / scales.astype(jnp.float32)[:, None]).astype(jnp.bfloat16)
    return (new_codes, new_accum)
```

```python
import jax
import jax.numpy as jnp
from jax import lax
from jax.experimental import pallas as pl
from jax.experimental.pallas import tpu as pltpu
from jax.sharding import PartitionSpec as P

LEARN_RATE = 0.1
ROOT_EPSILON = 1e-08
BLOCK = 512
CHUNK = 256
PIECES = 4
STAGES = 5
MESH = pl.DeviceIdType.MESH
NN = (((1,), (0,)), ((), ()))
NT = (((1,), (1,)), ((), ()))
BF = jnp.bfloat16
F32 = jnp.float32


def mul(a, b, dims):
    return lax.dot_general(a, b, dims, preferred_element_type=F32)


def turned(block):
    return block.astype(F32).T


def kernel(
    comm,
    matching, counts, codes, scales, accum, relations, edges, negatives,
    out_codes, out_accum,
    rows, src_t, query_t, rel_t, qg_t, g_t, hits, tall, rel_turned, spots,
    dg_acc, dg_own, sg_own, held2,
    xbuf, dg_mate_in, dg_far_in, dg_mate_out, dg_far_out,
    sg_mate_in, sg_far_in, sg_mate_out, sg_far_out,
    x_s, x_r, ag_s, ag_r, dm_s, dm_r, df_s, df_r, sm_s, sm_r, sf_s, sf_r, o_s, o_r,
):
    n_chunk = codes.shape[0] // CHUNK
    n_block = edges.shape[1] // BLOCK
    if comm:
        d = lax.axis_index("dom")
        r = lax.axis_index("rep")
    else:
        d = jnp.int32(0)
        r = jnp.int32(0)
    core = r % 2
    z_hi = r // 2
    mate = {"rep": r + 1 - 2 * core}

    def far(dz):
        return {"rep": ((z_hi + dz) % 4) * 2 + core}

    def chunk_of(dz, dc):
        return ((z_hi + dz) % 4) * 2 + (core if dc == 0 else 1 - core)

    near = [
        {"dom": d + 1 - 2 * (d % 2)},
        {"dom": d + 8 - 16 * ((d // 8) % 2)},
        {"dom": d + 3 - 2 * (d % 4)},
        {"dom": d + 24 - 16 * (d // 8)},
        {"dom": d + 4 - 8 * ((d // 4) % 2)},
    ]
    partner = jnp.bitwise_xor(matching[0], d)
    in_x = jnp.bitwise_and(partner, 3)
    in_z = jnp.bitwise_and(jnp.right_shift(partner, 2), 1)
    in_y = jnp.bitwise_and(jnp.right_shift(partner, 3), 3)
    wanted = [
        (in_x == 1) | (in_x == 2),
        (in_y == 1) | (in_y == 2),
        in_x >= 2,
        in_y >= 2,
        in_z == 1,
    ]
    wanted = [w.astype(F32) for w in wanted]

    def copy(src, dst, s, t, to):
        return pltpu.make_async_remote_copy(
            src_ref=src, dst_ref=dst, send_sem=s, recv_sem=t, device_id=to, device_id_type=MESH
        )

    def start(c):
        if comm:
            c.start()

    def got(c):
        if comm:
            c.wait_recv()

    def left(c):
        if comm:
            c.wait_send()

    if comm:
        barrier = pltpu.get_barrier_semaphore()
        for to in near + [mate, far(1), far(2), far(3)]:
            pl.semaphore_signal(barrier, inc=1, device_id=to, device_id_type=MESH)

    def piece_copy(which, held, j, p):
        part = held.at[pl.ds(p * (CHUNK // PIECES), CHUNK // PIECES)]
        st = (p + j) % STAGES
        return copy(part, xbuf.at[which, j, p], x_s.at[which, j, p], x_r.at[which, j, p], near[st])

    def start_round(which, held, j):
        for p in range(PIECES):
            start(piece_copy(which, held, j, p))

    def end_round(which, held, j):
        for p in range(PIECES):
            c = piece_copy(which, held, j, p)
            got(c)
            left(c)
            take = wanted[(p + j) % STAGES]
            part = pl.ds(p * (CHUNK // PIECES), CHUNK // PIECES)
            mine = held[part, :].astype(F32)
            theirs = xbuf[which, j, p].astype(F32)
            held[part, :] = jnp.where(
                jnp.full(mine.shape, take, F32) > 0.5, theirs, mine
            ).astype(BF)
            if j + 1 < STAGES:
                start(piece_copy(which, held, j + 1, p))

    def scale_row(k):
        return scales[:, pl.ds(pl.multiple_of(k * CHUNK, CHUNK), CHUNK)].astype(F32)

    def values_t(k):
        at = pl.multiple_of(k * CHUNK, CHUNK)
        return turned(codes[pl.ds(at, CHUNK), :]) * scale_row(k)

    rows[0] = values_t(r).T.astype(BF)
    if comm:
        pl.semaphore_wait(barrier, len(near) + 4)
    start_round(0, rows.at[0], 0)

    spots[...] = lax.broadcasted_iota(jnp.int32, spots.shape, 0).astype(F32).astype(BF)
    rel_turned[...] = turned(relations[...]).astype(BF)

    def tables(k, _):
        src_t[k] = values_t(k).astype(BF)
        return 0

    lax.fori_loop(0, n_chunk, tables, 0)

    def count_block(c, _):
        ids = negatives[pl.ds(c, 1), :]
        high = jnp.right_shift(ids, 8)
        low = jnp.bitwise_and(ids, CHUNK - 1)
        n = ids.shape[1]
        high_hot = jnp.where(
            lax.broadcasted_iota(jnp.int32, (n_chunk, n), 0) == high, 1.0, 0.0
        ).astype(BF)
        low_hot = jnp.where(
            lax.broadcasted_iota(jnp.int32, (CHUNK, n), 0) == low, 1.0, 0.0
        ).astype(BF)
        table = mul(high_hot, low_hot, NT) * (0.5 / n)
        for k in range(n_chunk):
            tall[...] = jnp.broadcast_to(table[k : k + 1, :], (128, CHUNK))
            hits[k, c] = tall[...].T.astype(BF)
        return 0

    lax.fori_loop(0, n_block, count_block, 0)

    def hot_rows(ids, k):
        local = jnp.where(jnp.right_shift(ids, 8) == k, jnp.bitwise_and(ids, CHUNK - 1), -1)
        local = local.astype(F32).astype(BF)
        return spots[...] == local

    one, zero = jnp.ones((), BF), jnp.zeros((), BF)

    def query_block(c, _):
        at = pl.ds(pl.multiple_of(c * BLOCK, BLOCK), BLOCK)
        src = edges[0:1, at]
        slot = lax.broadcasted_iota(jnp.int32, (1, BLOCK), 1) + c * BLOCK
        rel = jnp.where(slot < counts[0], edges[1:2, at], -1)
        n_rel = relations.shape[0]
        rel_hot = jnp.where(
            lax.broadcasted_iota(jnp.int32, (n_rel, BLOCK), 0) == rel, 1.0, 0.0
        ).astype(BF)
        rel_rows = mul(rel_turned[...], rel_hot, NN)
        found = jnp.zeros((CHUNK, BLOCK), F32)
        for k in range(n_chunk):
            found = found + mul(src_t[k], jnp.where(hot_rows(src, k), one, zero), NN)
        query_t[:, at] = (found * rel_rows).astype(BF)
        rel_t[:, at] = rel_rows.astype(BF)
        qg_t[:, at] = jnp.zeros((CHUNK, BLOCK), F32)
        return 0

    per = n_block // 4
    for j in range(4):
        lax.fori_loop(j * per, (j + 1) * per, query_block, 0)
        end_round(0, rows.at[0], j)
    end_round(0, rows.at[0], 4)

    ag = {}
    ag[1] = copy(rows.at[0], rows.at[1], ag_s.at[0], ag_r.at[1], mate)
    start(ag[1])
    for dz in (1, 3, 2):
        back = (4 - dz) % 4
        ag[2 * back] = copy(rows.at[0], rows.at[2 * back], ag_s.at[dz], ag_r.at[2 * back], far(dz))
        start(ag[2 * back])

    def relay(dz):
        got(ag[2 * dz])
        ag[2 * dz + 1] = copy(
            rows.at[2 * dz], rows.at[2 * dz + 1], ag_s.at[3 + dz], ag_r.at[2 * dz + 1], mate
        )
        start(ag[2 * dz + 1])

    def score_chunk(slot, k):
        there = rows[slot]
        half = there * jnp.asarray(0.5, BF)
        there_t = turned(there).astype(BF)
        dg_acc[...] = jnp.zeros_like(dg_acc)

        def block(c, _):
            at = pl.ds(pl.multiple_of(c * BLOCK, BLOCK), BLOCK)
            query = query_t[:, at]
            t = jnp.tanh(mul(half, query, NN))
            up = (t + 1.0).astype(BF)
            down = (t * 0.5 - 0.5).astype(BF)
            often = hits[k, c]
            neg = jnp.concatenate([often] * (BLOCK // 128), axis=1) * up
            coef = jnp.where(hot_rows(edges[2:3, at], k), neg + down, neg)
            qg_t[:, at] += mul(there_t, coef, NN)
            dg_acc[...] += mul(coef, query, NT)
            return 0

        lax.fori_loop(0, n_block, block, 0, unroll=2)
        return dg_acc[...]

    def reduce_pair(dz, run, own, mate_in, far_in, mate_out, far_out, m_s, m_r, f_s, f_r):
        to_mate = copy(mate_out.at[dz], mate_in.at[dz], m_s.at[dz], m_r.at[dz], mate)
        if dz == 0:
            own[...] = run(0, 0)
            mate_out[0] = run(0, 1).astype(BF)
            start(to_mate)
            return [to_mate]
        mate_out[dz] = run(dz, 1).astype(BF)
        start(to_mate)
        both = run(dz, 0)
        got(to_mate)
        far_out[dz - 1] = (both + mate_in[dz].astype(F32)).astype(BF)
        back = (4 - dz) % 4
        away = copy(far_out.at[dz - 1], far_in.at[back - 1], f_s.at[dz - 1], f_r.at[back - 1], far(dz))
        start(away)
        return [to_mate, away]

    def total(own, mate_in, far_in):
        whole = own[...] + mate_in[0].astype(F32)
        for j in range(3):
            whole = whole + far_in[j].astype(F32)
        return whole

    dg_refs = (dg_own, dg_mate_in, dg_far_in, dg_mate_out, dg_far_out, dm_s, dm_r, df_s, df_r)
    sg_refs = (sg_own, sg_mate_in, sg_far_in, sg_mate_out, sg_far_out, sm_s, sm_r, sf_s, sf_r)
    sent = []

    def run_scores(dz, dc):
        if dc == 1:
            got(ag[2 * dz + 1])
        return score_chunk(2 * dz + dc, chunk_of(dz, dc))

    dg_copies = {}
    for i, dz in enumerate((0, 1, 3, 2)):
        dg_copies[dz] = reduce_pair(dz, run_scores, *dg_refs)
        if i == 0:
            for other in (1, 3, 2):
                relay(other)

    def finish_query_grad(c, _):
        at = pl.ds(pl.multiple_of(c * BLOCK, BLOCK), BLOCK)
        g_t[:, at] = (qg_t[:, at] * rel_t[:, at].astype(F32)).astype(BF)
        return 0

    lax.fori_loop(0, n_block, finish_query_grad, 0)

    def run_source(dz, dc):
        k = chunk_of(dz, dc)
        dg_acc[...] = jnp.zeros_like(dg_acc)

        def block(c, _):
            at = pl.ds(pl.multiple_of(c * BLOCK, BLOCK), BLOCK)
            hot = jnp.where(hot_rows(edges[0:1, at], k), one, zero)
            dg_acc[...] += mul(hot, g_t[:, at], NT)
            return 0

        lax.fori_loop(0, n_block, block, 0, unroll=4)
        return dg_acc[...]

    sg_copies = {}
    for dz in (2, 1):
        sg_copies[dz] = reduce_pair(dz, run_source, *sg_refs)

    got(dg_copies[0][0])
    for dz in (1, 2, 3):
        got(dg_copies[dz][1])
    held2[...] = total(dg_own, dg_mate_in, dg_far_in).astype(BF)
    start_round(1, held2, 0)
    sg_copies[3] = reduce_pair(3, run_source, *sg_refs)
    end_round(1, held2, 0)
    sg_copies[0] = reduce_pair(0, run_source, *sg_refs)
    for j in range(1, STAGES):
        end_round(1, held2, j)

    got(sg_copies[0][0])
    for dz in (1, 2, 3):
        got(sg_copies[dz][1])
    grad_t = turned(total(sg_own, sg_mate_in, sg_far_in) + held2[...].astype(F32))
    here = pl.ds(pl.multiple_of(r * CHUNK, CHUNK), CHUNK)
    state = accum[:, here] + jnp.mean(grad_t * grad_t, axis=0, keepdims=True)
    out_accum[...] = state
    updated = values_t(r) - LEARN_RATE * grad_t / (jnp.sqrt(state) + ROOT_EPSILON)
    out_codes[here, :] = (updated / scale_row(r)).T.astype(BF)

    mine = out_codes.at[here]
    og = {1: copy(mine, mine, o_s.at[0], o_r.at[1], mate)}
    start(og[1])
    for dz in (2, 1, 3):
        back = (4 - dz) % 4
        og[2 * back] = copy(mine, mine, o_s.at[dz], o_r.at[2 * back], far(dz))
        start(og[2 * back])
    for dz in (1, 3, 2):
        got(og[2 * dz])
        theirs = out_codes.at[pl.ds(pl.multiple_of(chunk_of(dz, 0) * CHUNK, CHUNK), CHUNK)]
        og[2 * dz + 1] = copy(theirs, theirs, o_s.at[3 + dz], o_r.at[2 * dz + 1], mate)
        start(og[2 * dz + 1])
    for dc in (1, 3, 5, 7):
        got(og[dc])
    for c in list(og.values()) + list(ag.values()):
        left(c)
    for copies in list(dg_copies.values()) + list(sg_copies.values()):
        for c in copies:
            left(c)
    for c in sent:
        left(c)


def call(comm, matching, counts, codes, scales, accum, relations, edges, negatives):
    import functools

    n, width = codes.shape
    slots = edges.shape[1]
    n_chunk, n_block = n // CHUNK, slots // BLOCK
    share = (CHUNK, width)
    vmem = pl.BlockSpec(memory_space=pltpu.VMEM)
    smem = pl.BlockSpec(memory_space=pltpu.SMEM)
    sem = pltpu.SemaphoreType.DMA
    scratch = [
        pltpu.VMEM((n_chunk,) + share, BF),
        pltpu.VMEM((n_chunk, width, CHUNK), BF),
        pltpu.VMEM((width, slots), BF),
        pltpu.VMEM((width, slots), BF),
        pltpu.VMEM((width, slots), F32),
        pltpu.VMEM((width, slots), BF),
        pltpu.VMEM((n_chunk, n_block, CHUNK, 128), BF),
        pltpu.VMEM((128, CHUNK), F32),
        pltpu.VMEM((width, relations.shape[0]), BF),
        pltpu.VMEM((CHUNK, BLOCK), BF),
        pltpu.VMEM(share, F32),
        pltpu.VMEM(share, F32),
        pltpu.VMEM(share, F32),
        pltpu.VMEM(share, BF),
        pltpu.VMEM((2, STAGES, PIECES, CHUNK // PIECES, width), BF),
    ]
    for _ in range(2):
        scratch += [pltpu.VMEM((4,) + share, BF), pltpu.VMEM((3,) + share, BF)] * 2
    scratch += [sem((2, STAGES, PIECES)), sem((2, STAGES, PIECES)), sem((7,)), sem((8,))]
    scratch += [sem((4,)), sem((4,)), sem((3,)), sem((3,))] * 2
    scratch += [sem((7,)), sem((8,))]
    return pl.pallas_call(
        functools.partial(kernel, comm),
        out_shape=(
            jax.ShapeDtypeStruct((n, width), BF),
            jax.ShapeDtypeStruct((1, CHUNK), F32),
        ),
        in_specs=[smem, smem] + [vmem] * 6,
        out_specs=(vmem, vmem),
        scratch_shapes=scratch,
        compiler_params=pltpu.CompilerParams(
            collective_id=0 if comm else None,
            has_side_effects=True,
            vmem_limit_bytes=48 << 20,
        ),
    )(
        matching, counts, codes, scales.reshape(1, n), accum.reshape(1, n), relations, edges,
        negatives,
    )


def body(codes, scales, accum, relations, matching, edges, counts, negatives):
    new_codes, new_accum = call(
        True, matching, counts, codes, scales, accum, relations, edges, negatives
    )
    return new_codes, new_accum.reshape(-1)


def solution(mesh):
    placed = (
        P("dom", None),
        P("dom"),
        P("dom"),
        P(),
        P("dom"),
        P(None, ("dom", "rep")),
        P(("dom", "rep")),
        P(("dom", "rep"), None),
    )
    return jax.shard_map(
        body,
        mesh=mesh,
        in_specs=placed,
        out_specs=(P("dom", None), P(("dom", "rep"))),
        check_vma=False,
    )
```

```python
import functools

import jax
import jax.numpy as jnp
from jax import lax
from jax.experimental import pallas as pl
from jax.experimental.pallas import tpu as pltpu
from jax.sharding import PartitionSpec as P

LEARN_RATE = 0.1
ROOT_EPSILON = 1e-08
BLOCK = 512
CHUNK = 256
PIECES = ((0, 96), (96, 80), (176, 80))
MESH = pl.DeviceIdType.MESH
NN = (((1,), (0,)), ((), ()))
NT = (((1,), (1,)), ((), ()))
BF = jnp.bfloat16
F32 = jnp.float32


def mul(a, b, dims):
    return lax.dot_general(a, b, dims, preferred_element_type=F32)


def turned(block):
    return block.astype(F32).T


def kernel(
    comm,
    matching, counts, codes_hbm, scales_hbm, accum_hbm, relations_hbm, edges_hbm, negatives_hbm,
    out_codes, out_accum,
    share, codes, scales, accum, relations, edges, negatives,
    rows, rows_t, src_t, query_t, rel_t, g_t, coefs, hits, rel_turned, spots, spread,
    score_a, score_b, acc, dg_own, sg_own, held,
    xbuf, dg_mate_in, dg_far_in, dg_mate_out, dg_far_out,
    sg_mate_in, sg_far_in, sg_mate_out, sg_far_out,
    l_s, x_s, x_r, ag_s, ag_r, dm_s, dm_r, df_s, df_r, sm_s, sm_r, sf_s, sf_r, o_s, o_r,
):
    n_chunk = codes.shape[0] // CHUNK
    n_block = edges.shape[1] // BLOCK
    if comm:
        d = lax.axis_index("dom")
        r = lax.axis_index("rep")
    else:
        d = jnp.int32(0)
        r = jnp.int32(0)
    core = r % 2
    z_hi = r // 2
    mate = {"rep": r + 1 - 2 * core}

    def far(dz):
        return {"rep": ((z_hi + dz) % 4) * 2 + core}

    def pair_of(dz):
        return (z_hi + dz) % 4

    def span(i, n):
        return pl.ds(pl.multiple_of(i * n, n), n)

    near_x = [
        {"dom": d + 1 - 2 * (d % 2)},
        {"dom": d + 2 - 4 * ((d // 2) % 2)},
        {"dom": d + 3 - 2 * (d % 4)},
    ]
    near_z = [{"dom": d + 4 - 8 * ((d // 4) % 2)}]
    near_y = [
        {"dom": d + 8 - 16 * ((d // 8) % 2)},
        {"dom": d + 16 - 32 * ((d // 16) % 2)},
        {"dom": d + 24 - 16 * (d // 8)},
    ]
    partner = jnp.bitwise_xor(matching[0], d)
    in_x = jnp.bitwise_and(partner, 3)
    in_z = jnp.bitwise_and(jnp.right_shift(partner, 2), 1)
    in_y = jnp.bitwise_and(jnp.right_shift(partner, 3), 3)
    near = (near_y, near_x, near_z)
    wanted = [[(bits == i + 1).astype(F32) for i in range(3)] for bits in (in_y, in_x, in_z)]

    def copy(src, dst, s, t, to):
        return pltpu.make_async_remote_copy(
            src_ref=src, dst_ref=dst, send_sem=s, recv_sem=t, device_id=to, device_id_type=MESH
        )

    def start(*copies):
        if comm:
            for c in copies:
                c.start()

    def got(*copies):
        if comm:
            for c in copies:
                c.wait_recv()

    def left(*copies):
        if comm:
            for c in copies:
                c.wait_send()

    loads = [
        pltpu.make_async_copy(a, b, l_s.at[i])
        for i, (a, b) in enumerate(
            (
                (codes_hbm.at[span(r, CHUNK)], share),
                (scales_hbm, scales),
                (codes_hbm, codes),
                (relations_hbm, relations),
                (negatives_hbm, negatives),
                (edges_hbm, edges),
                (accum_hbm, accum),
            )
        )
    ]
    for c in loads:
        c.start()
    if comm:
        barrier = pltpu.get_barrier_semaphore()
        peers = near_x + near_y + near_z + [mate, far(1), far(2), far(3)]
        for to in peers:
            pl.semaphore_signal(barrier, inc=1, device_id=to, device_id_type=MESH)

    def piece_copies(which, j, p):
        at, n = PIECES[p]
        dim = (p + j) % 3
        return [
            copy(
                held.at[which, pl.ds(at, n)], xbuf.at[which, j, i, pl.ds(at, n)],
                x_s.at[which, j, p, i], x_r.at[which, j, p, i], to,
            )
            for i, to in enumerate(near[dim])
        ]

    def start_round(which, j):
        for p in range(3):
            start(*piece_copies(which, j, p))

    def end_round(which, j):
        for p, (at, n) in enumerate(PIECES):
            copies = piece_copies(which, j, p)
            got(*copies)
            left(*copies)
            kept = held[which, at : at + n, :].astype(F32)
            for i in range(len(copies)):
                take = jnp.full(kept.shape, wanted[(p + j) % 3][i], F32) > 0.5
                kept = jnp.where(take, xbuf[which, j, i, at : at + n, :].astype(F32), kept)
            held[which, at : at + n, :] = kept.astype(BF)
            if j < 2:
                start(*piece_copies(which, j + 1, p))

    def gather(slot, s, t, fixed=False):
        top, low = 0, CHUNK // 2

        def part(dz, at):
            return slot(dz, at, CHUNK // 2)

        def whole(dz):
            return slot(dz, 0, CHUNK)

        c = {}
        c["m0"] = copy(whole(0), whole(0), s.at[0], t.at[0], mate)
        c["a1t"] = copy(part(0, top), part(0, top) if fixed else part(3, top), s.at[1], t.at[1], far(1))
        c["a3b"] = copy(part(0, low), part(0, low) if fixed else part(1, low), s.at[2], t.at[2], far(3))
        c["a1b"] = copy(part(0, low), part(0, low) if fixed else part(3, low), s.at[3], t.at[3], far(1))
        c["a3t"] = copy(part(0, top), part(0, top) if fixed else part(1, top), s.at[4], t.at[4], far(3))
        c["f1"] = copy(part(3, top), part(3, top) if fixed else part(2, top), s.at[5], t.at[5], far(1))
        c["f3"] = copy(part(1, low), part(1, low) if fixed else part(2, low), s.at[6], t.at[6], far(3))
        for i, dz in enumerate((1, 3, 2)):
            c["m%d" % dz] = copy(whole(dz), whole(dz), s.at[7 + i], t.at[7 + i], mate)
        return c

    def gather_start(c):
        start(c["a1t"], c["a3b"], c["a1b"], c["a3t"], c["m0"])

    def gather_forward(c):
        got(c["a1t"])
        start(c["f1"])
        got(c["a3b"])
        start(c["f3"])

    def gather_mate(c):
        got(c["a3t"])
        start(c["m1"])
        got(c["a1b"])
        start(c["m3"])

    def gather_last(c):
        got(c["f1"], c["f3"])
        start(c["m2"])

    def scale_row(k):
        return scales[:, span(k, CHUNK)].astype(F32)

    loads[0].wait()
    loads[1].wait()
    share_t = turned(share[...]) * scale_row(r)
    held[0] = share_t.T.astype(BF)
    if comm:
        pl.semaphore_wait(barrier, len(peers))
    start_round(0, 0)

    for c in loads[2:]:
        c.wait()
    spots[...] = lax.broadcasted_iota(jnp.int32, spots.shape, 0).astype(F32).astype(BF)
    spread[...] = jnp.where(
        lax.broadcasted_iota(jnp.int32, spread.shape, 0)
        == jnp.right_shift(lax.broadcasted_iota(jnp.int32, spread.shape, 1), 7),
        1.0,
        0.0,
    ).astype(BF)
    rel_turned[...] = turned(relations[...]).astype(BF)
    one, zero = jnp.ones((), BF), jnp.zeros((), BF)

    def tables(k, _):
        src_t[k] = (turned(codes[span(k, CHUNK), :]) * scale_row(k)).astype(BF)
        return 0

    def count_block(c, _):
        ids = negatives[pl.ds(c, 1), :]
        n = ids.shape[1]
        low = jnp.bitwise_and(ids, CHUNK - 1).astype(F32).astype(BF)
        low_hot = jnp.where(spots[...] == low, one, zero)
        high_hot = jnp.where(
            lax.broadcasted_iota(jnp.int32, (128, n), 0) == jnp.right_shift(ids, 8), 1.0, 0.0
        ).astype(BF)
        table = (mul(low_hot, high_hot, NT) * (1.0 / n)).astype(BF)
        hits[c] = mul(table, spread[...], NN).astype(BF)
        return 0

    def hot_rows(ids, k):
        local = jnp.where(jnp.right_shift(ids, 8) == k, jnp.bitwise_and(ids, CHUNK - 1), -1)
        return spots[:, 0:BLOCK] == local.astype(F32).astype(BF)

    def query_block(c, _):
        at = span(c, BLOCK)
        src = edges[0:1, at]
        slot = lax.broadcasted_iota(jnp.int32, (1, BLOCK), 1) + c * BLOCK
        rel = jnp.where(slot < counts[0], edges[1:2, at], -1)
        n_rel = relations.shape[0]
        rel_hot = jnp.where(
            lax.broadcasted_iota(jnp.int32, (n_rel, BLOCK), 0) == rel, 1.0, 0.0
        ).astype(BF)
        rel_rows = mul(rel_turned[...], rel_hot, NN)
        found = jnp.zeros((CHUNK, BLOCK), F32)
        for k in range(n_chunk):
            found = found + mul(src_t[k], jnp.where(hot_rows(src, k), one, zero), NN)
        query_t[:, at] = (found * rel_rows).astype(BF)
        rel_t[:, at] = (rel_rows * 0.5).astype(BF)
        return 0

    lax.fori_loop(0, n_chunk, tables, 0, unroll=8)
    lax.fori_loop(0, n_block // 2, count_block, 0, unroll=4)
    end_round(0, 0)
    lax.fori_loop(n_block // 2, n_block, count_block, 0, unroll=4)
    end_round(0, 1)
    lax.fori_loop(0, n_block // 4, query_block, 0, unroll=2)
    end_round(0, 2)
    rows[0, span(core, CHUNK)] = held[0]

    def row_slot(dz, at, n):
        return rows.at[dz, pl.ds(pl.multiple_of(core * CHUNK + at, n), n)]

    ag = gather(row_slot, ag_s, ag_r)
    gather_start(ag)
    lax.fori_loop(n_block // 4, 3 * n_block // 4, query_block, 0, unroll=2)
    gather_forward(ag)
    lax.fori_loop(3 * n_block // 4, n_block, query_block, 0, unroll=2)

    def score_pair(dz):
        a = pair_of(dz)
        there = rows[dz]
        rows_t[dz] = turned(there).astype(BF)
        half = there * jnp.asarray(0.5, BF)
        acc[...] = jnp.zeros_like(acc)

        def score(c):
            return mul(half, query_t[:, span(c, BLOCK)], NN)

        def use(c, scores):
            at = span(c, BLOCK)
            dst = edges[2:3, at]
            for h in range(2):
                k = 2 * a + h
                t = jnp.tanh(scores[h * CHUNK : (h + 1) * CHUNK, :])
                up = (t + 1.0).astype(BF)
                down = (t - 1.0).astype(BF)
                often = hits[c, :, span(k, 128)]
                neg = jnp.concatenate([often] * (BLOCK // 128), axis=1) * up
                coefs[dz, h * CHUNK : (h + 1) * CHUNK, at] = jnp.where(
                    hot_rows(dst, k), neg + down, neg
                )
            acc[...] += mul(coefs[dz, :, at], query_t[:, at], NT)

        def two(i, _):
            score_b[...] = score(2 * i + 1)
            use(2 * i, score_a)
            score_a[...] = score(2 * i + 2)
            use(2 * i + 1, score_b)
            return 0

        score_a[...] = score(0)
        lax.fori_loop(0, n_block // 2 - 1, two, 0, unroll=3)
        score_b[...] = score(n_block - 1)
        use(n_block - 2, score_a)
        use(n_block - 1, score_b)

    def source_pair(dz):
        a = pair_of(dz)
        acc[...] = jnp.zeros_like(acc)

        def block(c, _):
            at = span(c, BLOCK)
            src = edges[0:1, at]
            hot = jnp.concatenate(
                [jnp.where(hot_rows(src, 2 * a + h), one, zero) for h in range(2)], axis=0
            )
            acc[...] += mul(hot, g_t[:, at], NT)
            return 0

        lax.fori_loop(0, n_block, block, 0, unroll=8)

    class Reduce:
        def __init__(self, own, mate_in, far_in, mate_out, far_out, m_s, m_r, f_s, f_r):
            self.own, self.mate_in, self.far_in = own, mate_in, far_in
            self.mate_out, self.far_out = mate_out, far_out
            self.m = [
                copy(mate_out.at[dz], mate_in.at[dz], m_s.at[dz], m_r.at[dz], mate)
                for dz in range(4)
            ]
            self.f = [None] + [
                copy(far_out.at[dz - 1], far_in.at[3 - dz], f_s.at[dz - 1], f_r.at[3 - dz], far(dz))
                for dz in (1, 2, 3)
            ]

        def give(self, dz):
            self.mate_out[dz] = acc[span(1 - core, CHUNK), :].astype(BF)
            start(self.m[dz])
            self.own[dz] = acc[span(core, CHUNK), :]

        def send(self, dz):
            got(self.m[dz])
            self.far_out[dz - 1] = (self.own[dz] + self.mate_in[dz].astype(F32)).astype(BF)
            start(self.f[dz])

        def total(self):
            got(self.m[0], *self.f[1:])
            whole = self.own[0] + self.mate_in[0].astype(F32)
            for j in range(3):
                whole = whole + self.far_in[j].astype(F32)
            return whole

        def done(self):
            left(*self.m, *self.f[1:])

    dg = Reduce(dg_own, dg_mate_in, dg_far_in, dg_mate_out, dg_far_out, dm_s, dm_r, df_s, df_r)
    sg = Reduce(sg_own, sg_mate_in, sg_far_in, sg_mate_out, sg_far_out, sm_s, sm_r, sf_s, sf_r)

    got(ag["m0"])
    score_pair(0)
    dg.give(0)
    gather_mate(ag)
    got(ag["m1"])
    score_pair(1)
    dg.give(1)
    gather_last(ag)
    got(ag["m2"])
    score_pair(2)
    dg.give(2)
    dg.send(1)
    got(ag["m3"])
    score_pair(3)
    dg.give(3)
    dg.send(2)

    def query_grad(c, _):
        at = span(c, BLOCK)
        whole = jnp.zeros((CHUNK, BLOCK), F32)
        for dz in range(4):
            whole = whole + mul(rows_t[dz], coefs[dz, :, at], NN)
        g_t[:, at] = (whole * rel_t[:, at].astype(F32)).astype(BF)
        return 0

    lax.fori_loop(0, n_block // 4, query_grad, 0, unroll=2)
    dg.send(3)
    lax.fori_loop(n_block // 4, n_block, query_grad, 0, unroll=2)
    source_pair(2)
    sg.give(2)
    source_pair(1)
    sg.give(1)
    sg.send(2)
    held[1] = (dg.total() * 0.5).astype(BF)
    start_round(1, 0)
    source_pair(3)
    sg.give(3)
    sg.send(1)
    source_pair(0)
    sg.give(0)
    sg.send(3)
    for j in range(3):
        end_round(1, j)

    grad_t = (sg.total() + held[1].astype(F32)).T
    state = accum[:, span(r, CHUNK)] + jnp.mean(grad_t * grad_t, axis=0, keepdims=True)
    out_accum[...] = state
    values_t = turned(share[...]) * scale_row(r)
    updated = values_t - LEARN_RATE * grad_t / (jnp.sqrt(state) + ROOT_EPSILON)
    out_codes[span(r, CHUNK), :] = (updated / scale_row(r)).T.astype(BF)

    def out_slot(dz, at, n):
        return out_codes.at[pl.ds(pl.multiple_of((pair_of(dz) * 2 + core) * CHUNK + at, n), n)]

    og = gather(out_slot, o_s, o_r, True)
    gather_start(og)
    gather_forward(og)
    gather_mate(og)
    gather_last(og)
    got(og["m0"], og["m1"], og["m3"], og["m2"])
    left(*og.values(), *ag.values())
    dg.done()
    sg.done()


def call(comm, matching, counts, codes, scales, accum, relations, edges, negatives):
    n, width = codes.shape
    slots = edges.shape[1]
    n_chunk, n_block = n // CHUNK, slots // BLOCK
    n_neg = negatives.shape[1]
    one = (CHUNK, width)
    vmem = pl.BlockSpec(memory_space=pltpu.VMEM)
    smem = pl.BlockSpec(memory_space=pltpu.SMEM)
    hbm = pl.BlockSpec(memory_space=pl.ANY)
    sem = pltpu.SemaphoreType.DMA
    scratch = [
        pltpu.VMEM(one, BF),
        pltpu.VMEM((n, width), BF),
        pltpu.VMEM((1, n), BF),
        pltpu.VMEM((1, n), F32),
        pltpu.VMEM(relations.shape, BF),
        pltpu.VMEM(edges.shape, jnp.int32),
        pltpu.VMEM(negatives.shape, jnp.int32),
        pltpu.VMEM((4, 2 * CHUNK, width), BF),
        pltpu.VMEM((4, width, 2 * CHUNK), BF),
        pltpu.VMEM((n_chunk, width, CHUNK), BF),
        pltpu.VMEM((width, slots), BF),
        pltpu.VMEM((width, slots), BF),
        pltpu.VMEM((width, slots), BF),
        pltpu.VMEM((4, 2 * CHUNK, slots), BF),
        pltpu.VMEM((n_block, CHUNK, n_chunk * 128), BF),
        pltpu.VMEM((width, relations.shape[0]), BF),
        pltpu.VMEM((CHUNK, n_neg), BF),
        pltpu.VMEM((128, n_chunk * 128), BF),
        pltpu.VMEM((2 * CHUNK, BLOCK), F32),
        pltpu.VMEM((2 * CHUNK, BLOCK), F32),
        pltpu.VMEM((2 * CHUNK, width), F32),
        pltpu.VMEM((4,) + one, F32),
        pltpu.VMEM((4,) + one, F32),
        pltpu.VMEM((2,) + one, BF),
        pltpu.VMEM((2, 3, 3) + one, BF),
    ]
    for _ in range(2):
        scratch += [pltpu.VMEM((4,) + one, BF), pltpu.VMEM((3,) + one, BF)] * 2
    scratch += [sem((7,)), sem((2, 3, 3, 3)), sem((2, 3, 3, 3)), sem((10,)), sem((10,))]
    scratch += [sem((4,)), sem((4,)), sem((3,)), sem((3,))] * 2
    scratch += [sem((10,)), sem((10,))]
    return pl.pallas_call(
        functools.partial(kernel, comm),
        out_shape=(
            jax.ShapeDtypeStruct((n, width), BF),
            jax.ShapeDtypeStruct((1, CHUNK), F32),
        ),
        in_specs=[smem, smem] + [hbm] * 6,
        out_specs=(vmem, vmem),
        scratch_shapes=scratch,
        compiler_params=pltpu.CompilerParams(
            collective_id=0 if comm else None,
            has_side_effects=True,
            vmem_limit_bytes=50 << 20,
        ),
    )(
        matching, counts, codes, scales.reshape(1, n), accum.reshape(1, n), relations, edges,
        negatives,
    )


def body(codes, scales, accum, relations, matching, edges, counts, negatives):
    new_codes, new_accum = call(
        True, matching, counts, codes, scales, accum, relations, edges, negatives
    )
    return new_codes, new_accum.reshape(-1)


def solution(mesh):
    placed = (
        P("dom", None),
        P("dom"),
        P("dom"),
        P(),
        P("dom"),
        P(None, ("dom", "rep")),
        P(("dom", "rep")),
        P(("dom", "rep"), None),
    )
    return jax.shard_map(
        body,
        mesh=mesh,
        in_specs=placed,
        out_specs=(P("dom", None), P(("dom", "rep"))),
        check_vma=False,
    )
```

```python
import functools

import jax
import jax.numpy as jnp
from jax import lax
from jax.experimental import pallas as pl
from jax.experimental.pallas import tpu as pltpu
from jax.sharding import PartitionSpec as P

LEARN_RATE = 0.1
ROOT_EPSILON = 1e-08
BLOCK = 512
CHUNK = 256
PIECES = 4
PIECE = CHUNK // PIECES
MESH = pl.DeviceIdType.MESH
NN = (((1,), (0,)), ((), ()))
NT = (((1,), (1,)), ((), ()))
BF = jnp.bfloat16
F32 = jnp.float32


def mul(a, b, dims):
    return lax.dot_general(a, b, dims, preferred_element_type=F32)


def turned(block):
    return block.astype(F32).T


def kernel(
    comm,
    matching, counts, codes_hbm, scales_hbm, accum_hbm, relations_hbm, edges_hbm, negatives_hbm,
    out_codes, out_accum,
    share, codes, scales, scale_col, accum_col, state_col, accum, relations, edges, negatives,
    rows, rows_t, src_t, query_t, rel_t, g_t, coefs, hits, rel_turned, spots, spread,
    score_a, score_b, acc, dg_own, sg_own, held,
    xbuf, dg_mate_in, dg_far_in, dg_mate_out, dg_far_out,
    sg_mate_in, sg_far_in, sg_mate_out, sg_far_out,
    l_s, x_s, x_r, ag_s, ag_r, dm_s, dm_r, df_s, df_r, sm_s, sm_r, sf_s, sf_r, o_s, o_r,
):
    n_chunk = codes.shape[0] // CHUNK
    n_block = edges.shape[1] // BLOCK
    if comm:
        d = lax.axis_index("dom")
        r = lax.axis_index("rep")
    else:
        d = jnp.int32(0)
        r = jnp.int32(0)
    core = r % 2
    z_hi = r // 2
    mate = {"rep": r + 1 - 2 * core}

    def far(dz):
        return {"rep": ((z_hi + dz) % 4) * 2 + core}

    def pair_of(dz):
        return (z_hi + dz) % 4

    def span(i, n):
        return pl.ds(pl.multiple_of(i * n, n), n)

    near_x = [
        {"dom": d + 1 - 2 * (d % 2)},
        {"dom": d + 2 - 4 * ((d // 2) % 2)},
        {"dom": d + 3 - 2 * (d % 4)},
    ]
    near_z = [{"dom": d + 4 - 8 * ((d // 4) % 2)}]
    near_y = [
        {"dom": d + 8 - 16 * ((d // 8) % 2)},
        {"dom": d + 16 - 32 * ((d // 16) % 2)},
        {"dom": d + 24 - 16 * (d // 8)},
    ]
    partner = jnp.bitwise_xor(matching[0], d)
    in_x = jnp.bitwise_and(partner, 3)
    in_z = jnp.bitwise_and(jnp.right_shift(partner, 2), 1)
    in_y = jnp.bitwise_and(jnp.right_shift(partner, 3), 3)
    near = (near_y, near_x, near_z)
    wanted = [[(bits == i + 1).astype(F32) for i in range(3)] for bits in (in_y, in_x, in_z)]

    def copy(src, dst, s, t, to):
        return pltpu.make_async_remote_copy(
            src_ref=src, dst_ref=dst, send_sem=s, recv_sem=t, device_id=to, device_id_type=MESH
        )

    def start(*copies):
        if comm:
            for c in copies:
                c.start()

    def got(*copies):
        if comm:
            for c in copies:
                c.wait_recv()

    def left(*copies):
        if comm:
            for c in copies:
                c.wait_send()

    loads = [
        pltpu.make_async_copy(a, b, l_s.at[i])
        for i, (a, b) in enumerate(
            (
                (codes_hbm.at[span(r, CHUNK)], share),
                (scales_hbm, scales),
                (codes_hbm, codes),
                (relations_hbm, relations),
                (negatives_hbm, negatives),
                (edges_hbm, edges),
                (accum_hbm, accum),
            )
        )
    ]
    for c in loads:
        c.start()
    if comm:
        barrier = pltpu.get_barrier_semaphore()
        peers = near_x + near_y + near_z + [mate, far(1), far(2), far(3)]
        for to in peers:
            pl.semaphore_signal(barrier, inc=1, device_id=to, device_id_type=MESH)

    def piece_copies(which, j, p):
        at = pl.ds(p * PIECE, PIECE)
        return [
            copy(
                held.at[which, at], xbuf.at[which, j, i, at],
                x_s.at[which, j, p, i], x_r.at[which, j, p, i], to,
            )
            for i, to in enumerate(near[order(j, p)])
        ]

    def order(j, p):
        return 2 if j == 2 else (p + j) % 2

    def exchange_start(which):
        for p in range(PIECES):
            start(*piece_copies(which, 0, p))

    def end_round(which, j, then=None):
        for p in range(PIECES):
            at = slice(p * PIECE, (p + 1) * PIECE)
            copies = piece_copies(which, j, p)
            got(*copies)
            left(*copies)
            kept = held[which, at, :].astype(F32)
            for i in range(len(copies)):
                take = jnp.full(kept.shape, wanted[order(j, p)][i], F32) > 0.5
                kept = jnp.where(take, xbuf[which, j, i, at, :].astype(F32), kept)
            held[which, at, :] = kept.astype(BF)
            if j < 2:
                start(*piece_copies(which, j + 1, p))
            else:
                then(p)

    def gather(slot, s, t, fixed=False):
        def part(dz, p):
            return slot(dz, p * PIECE, PIECE)

        def whole(dz):
            return slot(dz, 0, CHUNK)

        c = {}
        for p in range(PIECES):
            mine = part(0, p)
            c["up", p] = copy(mine, mine if fixed else part(3, p), s.at[p], t.at[p], far(1))
            c["down", p] = copy(mine, mine if fixed else part(1, p), s.at[4 + p], t.at[4 + p], far(3))
            c["mate", p] = copy(mine, mine, s.at[8 + p], t.at[8 + p], mate)
            via, to = (3, far(1)) if p < PIECES // 2 else (1, far(3))
            passing = part(via, p)
            c["on", p] = copy(
                passing, passing if fixed else part(2, p), s.at[12 + p], t.at[12 + p], to
            )
        for dz in (1, 2, 3):
            c["relay", dz] = copy(whole(dz), whole(dz), s.at[15 + dz], t.at[15 + dz], mate)
        return c

    def gather_piece(c, p):
        start(c["up", p], c["down", p], c["mate", p])

    def gather_forward(c):
        for p in range(PIECES):
            got(c["up" if p < PIECES // 2 else "down", p])
            start(c["on", p])

    def gather_mate(c):
        got(*[c["down", p] for p in range(PIECES // 2)])
        start(c["relay", 1])
        got(*[c["up", p] for p in range(PIECES // 2, PIECES)])
        start(c["relay", 3])

    def gather_last(c):
        got(*[c["on", p] for p in range(PIECES)])
        start(c["relay", 2])

    def scale_row(k):
        return scales[:, span(k, CHUNK)].astype(F32)

    for c in loads:
        c.wait()
    share_t = turned(share[...]) * scale_row(r)
    held[0] = share_t.T.astype(BF)
    spots[...] = lax.broadcasted_iota(jnp.int32, spots.shape, 0).astype(F32).astype(BF)
    spread[...] = jnp.where(
        lax.broadcasted_iota(jnp.int32, spread.shape, 0)
        == jnp.right_shift(lax.broadcasted_iota(jnp.int32, spread.shape, 1), 7),
        1.0,
        0.0,
    ).astype(BF)
    rel_turned[...] = turned(relations[...]).astype(BF)
    one, zero = jnp.ones((), BF), jnp.zeros((), BF)

    def tables(k, _):
        src_t[k] = (turned(codes[span(k, CHUNK), :]) * scale_row(k)).astype(BF)
        return 0

    def count_block(c, _):
        ids = negatives[pl.ds(c, 1), :]
        n = ids.shape[1]
        low = jnp.bitwise_and(ids, CHUNK - 1).astype(F32).astype(BF)
        low_hot = jnp.where(spots[...] == low, one, zero)
        high_hot = jnp.where(
            lax.broadcasted_iota(jnp.int32, (128, n), 0) == jnp.right_shift(ids, 8), 1.0, 0.0
        ).astype(BF)
        table = (mul(low_hot, high_hot, NT) * (1.0 / n)).astype(BF)
        hits[c] = mul(table, spread[...], NN).astype(BF)
        return 0

    def hot_rows(ids, k):
        local = jnp.where(jnp.right_shift(ids, 8) == k, jnp.bitwise_and(ids, CHUNK - 1), -1)
        return spots[:, 0:BLOCK] == local.astype(F32).astype(BF)

    def query_block(c, _):
        at = span(c, BLOCK)
        src = edges[0:1, at]
        slot = lax.broadcasted_iota(jnp.int32, (1, BLOCK), 1) + c * BLOCK
        rel = jnp.where(slot < counts[0], edges[1:2, at], -1)
        n_rel = relations.shape[0]
        rel_hot = jnp.where(
            lax.broadcasted_iota(jnp.int32, (n_rel, BLOCK), 0) == rel, 1.0, 0.0
        ).astype(BF)
        rel_rows = mul(rel_turned[...], rel_hot, NN)
        found = jnp.zeros((CHUNK, BLOCK), F32)
        for k in range(n_chunk):
            found = found + mul(src_t[k], jnp.where(hot_rows(src, k), one, zero), NN)
        query_t[:, at] = (found * rel_rows).astype(BF)
        rel_t[:, at] = (rel_rows * 0.5).astype(BF)
        return 0

    def row_slot(dz, at, n):
        return rows.at[dz, pl.ds(pl.multiple_of(core * CHUNK + at, n), n)]

    ag = gather(row_slot, ag_s, ag_r)

    def pass_on(p):
        at = pl.ds(pl.multiple_of(core * CHUNK + p * PIECE, PIECE), PIECE)
        rows[0, at] = held[0, p * PIECE : (p + 1) * PIECE, :]
        gather_piece(ag, p)

    lax.fori_loop(0, n_chunk, tables, 0, unroll=8)
    lax.fori_loop(0, n_block // 2, count_block, 0, unroll=4)
    if comm:
        pl.semaphore_wait(barrier, len(peers))
    exchange_start(0)
    lax.fori_loop(n_block // 2, n_block, count_block, 0, unroll=4)
    lax.fori_loop(0, n_block // 4, query_block, 0, unroll=2)
    end_round(0, 0)
    lax.fori_loop(n_block // 4, n_block // 2, query_block, 0, unroll=2)
    end_round(0, 1)
    scale_col[...] = jnp.broadcast_to(scale_row(r), (128, CHUNK)).T
    accum_col[...] = jnp.broadcast_to(accum[:, span(r, CHUNK)], (128, CHUNK)).T
    lax.fori_loop(n_block // 2, 3 * n_block // 4, query_block, 0, unroll=2)
    end_round(0, 2, pass_on)
    lax.fori_loop(3 * n_block // 4, n_block, query_block, 0, unroll=2)
    gather_forward(ag)

    def score_pair(dz):
        a = pair_of(dz)
        there = rows[dz]
        rows_t[dz] = turned(there).astype(BF)
        half = there * jnp.asarray(0.5, BF)
        acc[...] = jnp.zeros_like(acc)

        def score(c):
            return mul(half, query_t[:, span(c, BLOCK)], NN)

        def use(c, scores):
            at = span(c, BLOCK)
            dst = edges[2:3, at]
            for h in range(2):
                k = 2 * a + h
                t = jnp.tanh(scores[h * CHUNK : (h + 1) * CHUNK, :])
                up = (t + 1.0).astype(BF)
                down = (t - 1.0).astype(BF)
                often = hits[c, :, span(k, 128)]
                neg = jnp.concatenate([often] * (BLOCK // 128), axis=1) * up
                coefs[dz, h * CHUNK : (h + 1) * CHUNK, at] = jnp.where(
                    hot_rows(dst, k), neg + down, neg
                )
            acc[...] += mul(coefs[dz, :, at], query_t[:, at], NT)

        def two(i, _):
            score_b[...] = score(2 * i + 1)
            use(2 * i, score_a)
            score_a[...] = score(2 * i + 2)
            use(2 * i + 1, score_b)
            return 0

        score_a[...] = score(0)
        lax.fori_loop(0, n_block // 2 - 1, two, 0, unroll=3)
        score_b[...] = score(n_block - 1)
        use(n_block - 2, score_a)
        use(n_block - 1, score_b)

    def source_pair(dz):
        a = pair_of(dz)
        acc[...] = jnp.zeros_like(acc)

        def block(c, _):
            at = span(c, BLOCK)
            src = edges[0:1, at]
            hot = jnp.concatenate(
                [jnp.where(hot_rows(src, 2 * a + h), one, zero) for h in range(2)], axis=0
            )
            acc[...] += mul(hot, g_t[:, at], NT)
            return 0

        lax.fori_loop(0, n_block, block, 0, unroll=8)

    class Reduce:
        def __init__(self, own, mate_in, far_in, mate_out, far_out, m_s, m_r, f_s, f_r):
            self.own, self.mate_in, self.far_in = own, mate_in, far_in
            self.mate_out, self.far_out = mate_out, far_out
            self.m = [
                copy(mate_out.at[dz], mate_in.at[dz], m_s.at[dz], m_r.at[dz], mate)
                for dz in range(4)
            ]
            self.f = [None] + [
                copy(far_out.at[dz - 1], far_in.at[3 - dz], f_s.at[dz - 1], f_r.at[3 - dz], far(dz))
                for dz in (1, 2, 3)
            ]

        def give(self, dz):
            self.mate_out[dz] = acc[span(1 - core, CHUNK), :].astype(BF)
            start(self.m[dz])
            self.own[dz] = acc[span(core, CHUNK), :]

        def send(self, dz):
            got(self.m[dz])
            self.far_out[dz - 1] = (self.own[dz] + self.mate_in[dz].astype(F32)).astype(BF)
            start(self.f[dz])

        def total(self):
            got(self.m[0], *self.f[1:])
            whole = self.own[0] + self.mate_in[0].astype(F32)
            for j in range(3):
                whole = whole + self.far_in[j].astype(F32)
            return whole

        def done(self):
            left(*self.m, *self.f[1:])

    dg = Reduce(dg_own, dg_mate_in, dg_far_in, dg_mate_out, dg_far_out, dm_s, dm_r, df_s, df_r)
    sg = Reduce(sg_own, sg_mate_in, sg_far_in, sg_mate_out, sg_far_out, sm_s, sm_r, sf_s, sf_r)

    got(*[ag["mate", p] for p in range(PIECES)])
    score_pair(0)
    dg.give(0)
    gather_mate(ag)
    got(ag["relay", 1])
    score_pair(1)
    dg.give(1)
    gather_last(ag)
    got(ag["relay", 2])
    score_pair(2)
    dg.give(2)
    dg.send(1)
    got(ag["relay", 3])
    score_pair(3)
    dg.give(3)
    dg.send(2)

    def query_grad(c, _):
        at = span(c, BLOCK)
        whole = jnp.zeros((CHUNK, BLOCK), F32)
        for dz in range(4):
            whole = whole + mul(rows_t[dz], coefs[dz, :, at], NN)
        g_t[:, at] = (whole * rel_t[:, at].astype(F32)).astype(BF)
        return 0

    lax.fori_loop(0, n_block // 4, query_grad, 0, unroll=2)
    dg.send(3)
    lax.fori_loop(n_block // 4, n_block, query_grad, 0, unroll=2)
    source_pair(2)
    sg.give(2)
    source_pair(1)
    sg.give(1)
    sg.send(2)
    held[1] = (dg.total() * 0.5).astype(BF)
    exchange_start(1)
    source_pair(3)
    sg.give(3)
    sg.send(1)
    source_pair(0)
    sg.give(0)
    sg.send(3)
    def out_slot(dz, at, n):
        return out_codes.at[pl.ds(pl.multiple_of((pair_of(dz) * 2 + core) * CHUNK + at, n), n)]

    og = gather(out_slot, o_s, o_r, True)

    def wide(block):
        return jnp.concatenate([block, block], axis=1)

    def update(p):
        at = slice(p * PIECE, (p + 1) * PIECE)
        here = pl.ds(pl.multiple_of(r * CHUNK + p * PIECE, PIECE), PIECE)
        grad = acc[at, :] + held[1, at, :].astype(F32)
        state = accum_col[at, :] + jnp.mean(grad * grad, axis=1, keepdims=True)
        state_col[at, :] = state
        scale = wide(scale_col[at, :])
        values = codes[here, :].astype(F32) * scale
        updated = values - LEARN_RATE * grad / wide(jnp.sqrt(state) + ROOT_EPSILON)
        out_codes[here, :] = (updated / scale).astype(BF)
        gather_piece(og, p)

    end_round(1, 0)
    end_round(1, 1)
    acc[0:CHUNK, :] = sg.total()
    end_round(1, 2, update)
    gather_forward(og)
    gather_mate(og)
    out_accum[...] = state_col[...].T[0:1, :]
    gather_last(og)
    got(*[og["mate", p] for p in range(PIECES)], *[og["relay", dz] for dz in (1, 3, 2)])
    left(*og.values(), *ag.values())
    dg.done()
    sg.done()


def call(comm, matching, counts, codes, scales, accum, relations, edges, negatives):
    n, width = codes.shape
    slots = edges.shape[1]
    n_chunk, n_block = n // CHUNK, slots // BLOCK
    n_neg = negatives.shape[1]
    one = (CHUNK, width)
    vmem = pl.BlockSpec(memory_space=pltpu.VMEM)
    smem = pl.BlockSpec(memory_space=pltpu.SMEM)
    hbm = pl.BlockSpec(memory_space=pl.ANY)
    sem = pltpu.SemaphoreType.DMA
    scratch = [
        pltpu.VMEM(one, BF),
        pltpu.VMEM((n, width), BF),
        pltpu.VMEM((1, n), BF),
        pltpu.VMEM((CHUNK, 128), F32),
        pltpu.VMEM((CHUNK, 128), F32),
        pltpu.VMEM((CHUNK, 128), F32),
        pltpu.VMEM((1, n), F32),
        pltpu.VMEM(relations.shape, BF),
        pltpu.VMEM(edges.shape, jnp.int32),
        pltpu.VMEM(negatives.shape, jnp.int32),
        pltpu.VMEM((4, 2 * CHUNK, width), BF),
        pltpu.VMEM((4, width, 2 * CHUNK), BF),
        pltpu.VMEM((n_chunk, width, CHUNK), BF),
        pltpu.VMEM((width, slots), BF),
        pltpu.VMEM((width, slots), BF),
        pltpu.VMEM((width, slots), BF),
        pltpu.VMEM((4, 2 * CHUNK, slots), BF),
        pltpu.VMEM((n_block, CHUNK, n_chunk * 128), BF),
        pltpu.VMEM((width, relations.shape[0]), BF),
        pltpu.VMEM((CHUNK, n_neg), BF),
        pltpu.VMEM((128, n_chunk * 128), BF),
        pltpu.VMEM((2 * CHUNK, BLOCK), F32),
        pltpu.VMEM((2 * CHUNK, BLOCK), F32),
        pltpu.VMEM((2 * CHUNK, width), F32),
        pltpu.VMEM((4,) + one, F32),
        pltpu.VMEM((4,) + one, F32),
        pltpu.VMEM((2,) + one, BF),
        pltpu.VMEM((2, 3, 3) + one, BF),
    ]
    for _ in range(2):
        scratch += [pltpu.VMEM((4,) + one, BF), pltpu.VMEM((3,) + one, BF)] * 2
    scratch += [sem((7,)), sem((2, 3, PIECES, 3)), sem((2, 3, PIECES, 3)), sem((19,)), sem((19,))]
    scratch += [sem((4,)), sem((4,)), sem((3,)), sem((3,))] * 2
    scratch += [sem((19,)), sem((19,))]
    return pl.pallas_call(
        functools.partial(kernel, comm),
        out_shape=(
            jax.ShapeDtypeStruct((n, width), BF),
            jax.ShapeDtypeStruct((1, CHUNK), F32),
        ),
        in_specs=[smem, smem] + [hbm] * 6,
        out_specs=(vmem, vmem),
        scratch_shapes=scratch,
        compiler_params=pltpu.CompilerParams(
            collective_id=0 if comm else None,
            has_side_effects=True,
            vmem_limit_bytes=58 << 20,
        ),
    )(
        matching, counts, codes, scales.reshape(1, n), accum.reshape(1, n), relations, edges,
        negatives,
    )


def body(codes, scales, accum, relations, matching, edges, counts, negatives):
    new_codes, new_accum = call(
        True, matching, counts, codes, scales, accum, relations, edges, negatives
    )
    return new_codes, new_accum.reshape(-1)


def solution(mesh):
    placed = (
        P("dom", None),
        P("dom"),
        P("dom"),
        P(),
        P("dom"),
        P(None, ("dom", "rep")),
        P(("dom", "rep")),
        P(("dom", "rep"), None),
    )
    return jax.shard_map(
        body,
        mesh=mesh,
        in_specs=placed,
        out_specs=(P("dom", None), P(("dom", "rep"))),
        check_vma=False,
    )
```

```python
import functools

import jax
import jax.numpy as jnp
from jax import lax
from jax.experimental import pallas as pl
from jax.experimental.pallas import tpu as pltpu
from jax.sharding import PartitionSpec as P

LEARN_RATE = 0.1
ROOT_EPSILON = 1e-08
BLOCK = 512
CHUNK = 256
PIECES = 4
PIECE = CHUNK // PIECES
MESH = pl.DeviceIdType.MESH
NN = (((1,), (0,)), ((), ()))
NT = (((1,), (1,)), ((), ()))
BF = jnp.bfloat16
F32 = jnp.float32


def mul(a, b, dims):
    return lax.dot_general(a, b, dims, preferred_element_type=F32)


def turned(block):
    return block.astype(F32).T


def kernel(
    comm,
    matching, counts, codes_hbm, scales_hbm, accum_hbm, relations_hbm, edges_hbm, negatives_hbm,
    out_codes, out_accum,
    share, codes, scales, scale_col, accum_col, state_col, accum, relations, edges, negatives,
    rows, rows_t, src_t, query_t, rel_t, g_t, coefs, hits, rel_turned, spots, spread,
    score_a, score_b, acc, dg_own, sg_own, held,
    xbuf, dg_mate_in, dg_far_in, dg_mate_out, dg_far_out,
    sg_mate_in, sg_far_in, sg_mate_out, sg_far_out,
    l_s, x_s, x_r, ag_s, ag_r, dm_s, dm_r, df_s, df_r, sm_s, sm_r, sf_s, sf_r, o_s, o_r,
):
    n_chunk = codes.shape[0] // CHUNK
    n_block = edges.shape[1] // BLOCK
    if comm:
        d = lax.axis_index("dom")
        r = lax.axis_index("rep")
    else:
        d = jnp.int32(0)
        r = jnp.int32(0)
    core = r % 2
    z_hi = r // 2
    mate = {"rep": r + 1 - 2 * core}

    def far(dz):
        return {"rep": ((z_hi + dz) % 4) * 2 + core}

    def pair_of(dz):
        return (z_hi + dz) % 4

    def span(i, n):
        return pl.ds(pl.multiple_of(i * n, n), n)

    near_x = [
        {"dom": d + 1 - 2 * (d % 2)},
        {"dom": d + 2 - 4 * ((d // 2) % 2)},
        {"dom": d + 3 - 2 * (d % 4)},
    ]
    near_z = [{"dom": d + 4 - 8 * ((d // 4) % 2)}]
    near_y = [
        {"dom": d + 8 - 16 * ((d // 8) % 2)},
        {"dom": d + 16 - 32 * ((d // 16) % 2)},
        {"dom": d + 24 - 16 * (d // 8)},
    ]
    partner = jnp.bitwise_xor(matching[0], d)
    in_x = jnp.bitwise_and(partner, 3)
    in_z = jnp.bitwise_and(jnp.right_shift(partner, 2), 1)
    in_y = jnp.bitwise_and(jnp.right_shift(partner, 3), 3)
    near = (near_y, near_x, near_z)
    wanted = [[(bits == i + 1).astype(F32) for i in range(3)] for bits in (in_y, in_x, in_z)]

    def copy(src, dst, s, t, to):
        return pltpu.make_async_remote_copy(
            src_ref=src, dst_ref=dst, send_sem=s, recv_sem=t, device_id=to, device_id_type=MESH
        )

    def start(*copies):
        if comm:
            for c in copies:
                c.start()

    def got(*copies):
        if comm:
            for c in copies:
                c.wait_recv()

    def left(*copies):
        if comm:
            for c in copies:
                c.wait_send()

    loads = [
        pltpu.make_async_copy(a, b, l_s.at[i])
        for i, (a, b) in enumerate(
            (
                (codes_hbm.at[span(r, CHUNK)], share),
                (scales_hbm, scales),
                (codes_hbm, codes),
                (relations_hbm, relations),
                (negatives_hbm, negatives),
                (edges_hbm, edges),
                (accum_hbm, accum),
            )
        )
    ]
    for c in loads:
        c.start()
    if comm:
        barrier = pltpu.get_barrier_semaphore()
        peers = near_x + near_y + near_z + [mate, far(1), far(2), far(3)]
        for to in peers:
            pl.semaphore_signal(barrier, inc=1, device_id=to, device_id_type=MESH)

    def piece_copies(which, j, p):
        at = pl.ds(p * PIECE, PIECE)
        return [
            copy(
                held.at[which, at], xbuf.at[which, j, i, at],
                x_s.at[which, j, p, i], x_r.at[which, j, p, i], to,
            )
            for i, to in enumerate(near[order(j, p)])
        ]

    def order(j, p):
        return 2 if j == 2 else (p + j) % 2

    def exchange_start(which):
        for p in range(PIECES):
            start(*piece_copies(which, 0, p))

    def end_round(which, j, then=None):
        for p in range(PIECES):
            at = slice(p * PIECE, (p + 1) * PIECE)
            copies = piece_copies(which, j, p)
            got(*copies)
            left(*copies)
            kept = held[which, at, :].astype(F32)
            for i in range(len(copies)):
                take = jnp.full(kept.shape, wanted[order(j, p)][i], F32) > 0.5
                kept = jnp.where(take, xbuf[which, j, i, at, :].astype(F32), kept)
            held[which, at, :] = kept.astype(BF)
            if j < 2:
                start(*piece_copies(which, j + 1, p))
            else:
                then(p)

    def gather(slot, s, t, fixed=False):
        def part(dz, p):
            return slot(dz, p * PIECE, PIECE)

        def whole(dz):
            return slot(dz, 0, CHUNK)

        c = {}
        for p in range(PIECES):
            mine = part(0, p)
            c["up", p] = copy(mine, mine if fixed else part(3, p), s.at[p], t.at[p], far(1))
            c["down", p] = copy(mine, mine if fixed else part(1, p), s.at[4 + p], t.at[4 + p], far(3))
            c["mate", p] = copy(mine, mine, s.at[8 + p], t.at[8 + p], mate)
            via, to = (3, far(1)) if p < PIECES // 2 else (1, far(3))
            passing = part(via, p)
            c["on", p] = copy(
                passing, passing if fixed else part(2, p), s.at[12 + p], t.at[12 + p], to
            )
        for dz in (1, 2, 3):
            c["relay", dz] = copy(whole(dz), whole(dz), s.at[15 + dz], t.at[15 + dz], mate)
        return c

    def gather_piece(c, p):
        start(c["up", p], c["down", p], c["mate", p])

    def gather_forward(c):
        for p in range(PIECES):
            got(c["up" if p < PIECES // 2 else "down", p])
            start(c["on", p])

    def gather_mate(c):
        got(*[c["down", p] for p in range(PIECES // 2)])
        start(c["relay", 1])
        got(*[c["up", p] for p in range(PIECES // 2, PIECES)])
        start(c["relay", 3])

    def gather_last(c):
        got(*[c["on", p] for p in range(PIECES)])
        start(c["relay", 2])

    def scale_row(k):
        return scales[:, span(k, CHUNK)].astype(F32)

    for c in loads:
        c.wait()
    share_t = turned(share[...]) * scale_row(r)
    held[0] = share_t.T.astype(BF)
    spots[...] = lax.broadcasted_iota(jnp.int32, spots.shape, 0).astype(F32).astype(BF)
    spread[...] = jnp.where(
        lax.broadcasted_iota(jnp.int32, spread.shape, 0)
        == jnp.right_shift(lax.broadcasted_iota(jnp.int32, spread.shape, 1), 7),
        1.0,
        0.0,
    ).astype(BF)
    rel_turned[...] = turned(relations[...]).astype(BF)
    one, zero = jnp.ones((), BF), jnp.zeros((), BF)

    def tables(k, _):
        src_t[k] = (turned(codes[span(k, CHUNK), :]) * scale_row(k)).astype(BF)
        return 0

    def count_block(c, _):
        ids = negatives[pl.ds(c, 1), :]
        n = ids.shape[1]
        low = jnp.bitwise_and(ids, CHUNK - 1).astype(F32).astype(BF)
        low_hot = jnp.where(spots[...] == low, one, zero)
        high_hot = jnp.where(
            lax.broadcasted_iota(jnp.int32, (128, n), 0) == jnp.right_shift(ids, 8), 1.0, 0.0
        ).astype(BF)
        table = (mul(low_hot, high_hot, NT) * (1.0 / n)).astype(BF)
        hits[c] = mul(table, spread[...], NN).astype(BF)
        return 0

    def hot_rows(ids, k):
        local = jnp.where(jnp.right_shift(ids, 8) == k, jnp.bitwise_and(ids, CHUNK - 1), -1)
        return spots[:, 0:BLOCK] == local.astype(F32).astype(BF)

    def query_block(c, _):
        at = span(c, BLOCK)
        src = edges[0:1, at]
        slot = lax.broadcasted_iota(jnp.int32, (1, BLOCK), 1) + c * BLOCK
        rel = jnp.where(slot < counts[0], edges[1:2, at], -1)
        n_rel = relations.shape[0]
        rel_hot = jnp.where(
            lax.broadcasted_iota(jnp.int32, (n_rel, BLOCK), 0) == rel, 1.0, 0.0
        ).astype(BF)
        rel_rows = mul(rel_turned[...], rel_hot, NN)
        found = jnp.zeros((CHUNK, BLOCK), F32)
        for k in range(n_chunk):
            found = found + mul(src_t[k], jnp.where(hot_rows(src, k), one, zero), NN)
        query_t[:, at] = (found * rel_rows).astype(BF)
        rel_t[:, at] = (rel_rows * 0.5).astype(BF)
        return 0

    def row_slot(dz, at, n):
        return rows.at[dz, pl.ds(pl.multiple_of(core * CHUNK + at, n), n)]

    ag = gather(row_slot, ag_s, ag_r)

    def pass_on(p):
        at = pl.ds(pl.multiple_of(core * CHUNK + p * PIECE, PIECE), PIECE)
        rows[0, at] = held[0, p * PIECE : (p + 1) * PIECE, :]
        gather_piece(ag, p)

    lax.fori_loop(0, n_chunk, tables, 0, unroll=8)
    lax.fori_loop(0, n_block // 2, count_block, 0, unroll=4)
    if comm:
        pl.semaphore_wait(barrier, len(peers))
    exchange_start(0)
    lax.fori_loop(n_block // 2, n_block, count_block, 0, unroll=4)
    lax.fori_loop(0, n_block // 4, query_block, 0, unroll=2)
    end_round(0, 0)
    lax.fori_loop(n_block // 4, n_block // 2, query_block, 0, unroll=2)
    end_round(0, 1)
    scale_col[...] = jnp.broadcast_to(scale_row(r), (128, CHUNK)).T
    accum_col[...] = jnp.broadcast_to(accum[:, span(r, CHUNK)], (128, CHUNK)).T
    lax.fori_loop(n_block // 2, 3 * n_block // 4, query_block, 0, unroll=2)
    end_round(0, 2, pass_on)
    lax.fori_loop(3 * n_block // 4, n_block, query_block, 0, unroll=2)
    gather_forward(ag)

    def score_pair(dz):
        a = pair_of(dz)
        there = rows[dz]
        rows_t[dz] = turned(there).astype(BF)
        half = there * jnp.asarray(0.5, BF)
        acc[...] = jnp.zeros_like(acc)

        def score(c):
            return mul(half, query_t[:, span(c, BLOCK)], NN)

        def use(c, scores):
            at = span(c, BLOCK)
            dst = edges[2:3, at]
            for h in range(2):
                k = 2 * a + h
                t = jnp.tanh(scores[h * CHUNK : (h + 1) * CHUNK, :])
                up = (t + 1.0).astype(BF)
                down = (t - 1.0).astype(BF)
                often = hits[c, :, span(k, 128)]
                neg = jnp.concatenate([often] * (BLOCK // 128), axis=1) * up
                coefs[dz, h * CHUNK : (h + 1) * CHUNK, at] = jnp.where(
                    hot_rows(dst, k), neg + down, neg
                )
            acc[...] += mul(coefs[dz, :, at], query_t[:, at], NT)

        def two(i, _):
            score_b[...] = score(2 * i + 1)
            use(2 * i, score_a)
            score_a[...] = score(2 * i + 2)
            use(2 * i + 1, score_b)
            return 0

        score_a[...] = score(0)
        lax.fori_loop(0, n_block // 2 - 1, two, 0, unroll=3)
        score_b[...] = score(n_block - 1)
        use(n_block - 2, score_a)
        use(n_block - 1, score_b)

    def source_pair(dz):
        a = pair_of(dz)
        acc[...] = jnp.zeros_like(acc)

        def block(c, _):
            at = span(c, BLOCK)
            src = edges[0:1, at]
            hot = jnp.concatenate(
                [jnp.where(hot_rows(src, 2 * a + h), one, zero) for h in range(2)], axis=0
            )
            acc[...] += mul(hot, g_t[:, at], NT)
            return 0

        lax.fori_loop(0, n_block, block, 0, unroll=8)

    class Reduce:
        def __init__(self, own, mate_in, far_in, mate_out, far_out, m_s, m_r, f_s, f_r):
            self.own, self.mate_in, self.far_in = own, mate_in, far_in
            self.mate_out, self.far_out = mate_out, far_out
            self.m = [
                copy(mate_out.at[dz], mate_in.at[dz], m_s.at[dz], m_r.at[dz], mate)
                for dz in range(4)
            ]
            self.f = [None] + [
                copy(far_out.at[dz - 1], far_in.at[3 - dz], f_s.at[dz - 1], f_r.at[3 - dz], far(dz))
                for dz in (1, 2, 3)
            ]

        def give(self, dz):
            self.mate_out[dz] = acc[span(1 - core, CHUNK), :].astype(BF)
            start(self.m[dz])
            self.own[dz] = acc[span(core, CHUNK), :]

        def send(self, dz):
            got(self.m[dz])
            self.far_out[dz - 1] = (self.own[dz] + self.mate_in[dz].astype(F32)).astype(BF)
            start(self.f[dz])

        def total(self):
            got(self.m[0], *self.f[1:])
            whole = self.own[0] + self.mate_in[0].astype(F32)
            for j in range(3):
                whole = whole + self.far_in[j].astype(F32)
            return whole

        def done(self):
            left(*self.m, *self.f[1:])

    dg = Reduce(dg_own, dg_mate_in, dg_far_in, dg_mate_out, dg_far_out, dm_s, dm_r, df_s, df_r)
    sg = Reduce(sg_own, sg_mate_in, sg_far_in, sg_mate_out, sg_far_out, sm_s, sm_r, sf_s, sf_r)

    got(*[ag["mate", p] for p in range(PIECES)])
    score_pair(0)
    dg.give(0)
    gather_mate(ag)
    got(ag["relay", 1])
    score_pair(1)
    dg.give(1)
    gather_last(ag)
    got(ag["relay", 2])
    score_pair(2)
    dg.give(2)
    dg.send(1)
    got(ag["relay", 3])
    score_pair(3)
    dg.give(3)
    dg.send(2)

    def query_grad(c, _):
        at = span(c, BLOCK)
        whole = jnp.zeros((CHUNK, BLOCK), F32)
        for dz in range(4):
            whole = whole + mul(rows_t[dz], coefs[dz, :, at], NN)
        g_t[:, at] = (whole * rel_t[:, at].astype(F32)).astype(BF)
        return 0

    lax.fori_loop(0, n_block // 4, query_grad, 0, unroll=2)
    dg.send(3)
    lax.fori_loop(n_block // 4, n_block, query_grad, 0, unroll=2)
    source_pair(2)
    sg.give(2)
    source_pair(1)
    sg.give(1)
    sg.send(2)
    source_pair(3)
    sg.give(3)
    sg.send(1)
    source_pair(0)
    sg.give(0)
    sg.send(3)
    held[1] = (dg.total() * 0.5).astype(BF)
    exchange_start(1)
    def out_slot(dz, at, n):
        return out_codes.at[pl.ds(pl.multiple_of((pair_of(dz) * 2 + core) * CHUNK + at, n), n)]

    og = gather(out_slot, o_s, o_r, True)

    def wide(block):
        return jnp.concatenate([block, block], axis=1)

    def update(p):
        at = slice(p * PIECE, (p + 1) * PIECE)
        here = pl.ds(pl.multiple_of(r * CHUNK + p * PIECE, PIECE), PIECE)
        grad = acc[at, :] + held[1, at, :].astype(F32)
        state = accum_col[at, :] + jnp.mean(grad * grad, axis=1, keepdims=True)
        state_col[at, :] = state
        scale = wide(scale_col[at, :])
        values = codes[here, :].astype(F32) * scale
        updated = values - LEARN_RATE * grad / wide(jnp.sqrt(state) + ROOT_EPSILON)
        out_codes[here, :] = (updated / scale).astype(BF)
        gather_piece(og, p)

    end_round(1, 0)
    end_round(1, 1)
    acc[0:CHUNK, :] = sg.total()
    end_round(1, 2, update)
    gather_forward(og)
    gather_mate(og)
    out_accum[...] = state_col[...].T[0:1, :]
    gather_last(og)
    got(*[og["mate", p] for p in range(PIECES)], *[og["relay", dz] for dz in (1, 3, 2)])
    left(*og.values(), *ag.values())
    dg.done()
    sg.done()


def call(comm, matching, counts, codes, scales, accum, relations, edges, negatives):
    n, width = codes.shape
    slots = edges.shape[1]
    n_chunk, n_block = n // CHUNK, slots // BLOCK
    n_neg = negatives.shape[1]
    one = (CHUNK, width)
    vmem = pl.BlockSpec(memory_space=pltpu.VMEM)
    smem = pl.BlockSpec(memory_space=pltpu.SMEM)
    hbm = pl.BlockSpec(memory_space=pl.ANY)
    sem = pltpu.SemaphoreType.DMA
    scratch = [
        pltpu.VMEM(one, BF),
        pltpu.VMEM((n, width), BF),
        pltpu.VMEM((1, n), BF),
        pltpu.VMEM((CHUNK, 128), F32),
        pltpu.VMEM((CHUNK, 128), F32),
        pltpu.VMEM((CHUNK, 128), F32),
        pltpu.VMEM((1, n), F32),
        pltpu.VMEM(relations.shape, BF),
        pltpu.VMEM(edges.shape, jnp.int32),
        pltpu.VMEM(negatives.shape, jnp.int32),
        pltpu.VMEM((4, 2 * CHUNK, width), BF),
        pltpu.VMEM((4, width, 2 * CHUNK), BF),
        pltpu.VMEM((n_chunk, width, CHUNK), BF),
        pltpu.VMEM((width, slots), BF),
        pltpu.VMEM((width, slots), BF),
        pltpu.VMEM((width, slots), BF),
        pltpu.VMEM((4, 2 * CHUNK, slots), BF),
        pltpu.VMEM((n_block, CHUNK, n_chunk * 128), BF),
        pltpu.VMEM((width, relations.shape[0]), BF),
        pltpu.VMEM((CHUNK, n_neg), BF),
        pltpu.VMEM((128, n_chunk * 128), BF),
        pltpu.VMEM((2 * CHUNK, BLOCK), F32),
        pltpu.VMEM((2 * CHUNK, BLOCK), F32),
        pltpu.VMEM((2 * CHUNK, width), F32),
        pltpu.VMEM((4,) + one, F32),
        pltpu.VMEM((4,) + one, F32),
        pltpu.VMEM((2,) + one, BF),
        pltpu.VMEM((2, 3, 3) + one, BF),
    ]
    for _ in range(2):
        scratch += [pltpu.VMEM((4,) + one, BF), pltpu.VMEM((3,) + one, BF)] * 2
    scratch += [sem((7,)), sem((2, 3, PIECES, 3)), sem((2, 3, PIECES, 3)), sem((19,)), sem((19,))]
    scratch += [sem((4,)), sem((4,)), sem((3,)), sem((3,))] * 2
    scratch += [sem((19,)), sem((19,))]
    return pl.pallas_call(
        functools.partial(kernel, comm),
        out_shape=(
            jax.ShapeDtypeStruct((n, width), BF),
            jax.ShapeDtypeStruct((1, CHUNK), F32),
        ),
        in_specs=[smem, smem] + [hbm] * 6,
        out_specs=(vmem, vmem),
        scratch_shapes=scratch,
        compiler_params=pltpu.CompilerParams(
            collective_id=0 if comm else None,
            has_side_effects=True,
            vmem_limit_bytes=58 << 20,
        ),
    )(
        matching, counts, codes, scales.reshape(1, n), accum.reshape(1, n), relations, edges,
        negatives,
    )


def body(codes, scales, accum, relations, matching, edges, counts, negatives):
    new_codes, new_accum = call(
        True, matching, counts, codes, scales, accum, relations, edges, negatives
    )
    return new_codes, new_accum.reshape(-1)


def solution(mesh):
    placed = (
        P("dom", None),
        P("dom"),
        P("dom"),
        P(),
        P("dom"),
        P(None, ("dom", "rep")),
        P(("dom", "rep")),
        P(("dom", "rep"), None),
    )
    return jax.shard_map(
        body,
        mesh=mesh,
        in_specs=placed,
        out_specs=(P("dom", None), P(("dom", "rep"))),
        check_vma=False,
    )
```
